32 devices in a mesh: groups: 2 (over y), chan: 16 (over z, x, core).
Axes of the slice: x: 2, y: 2, z: 4, core: 2. Of those that a mesh axis runs over, the one named last changes fastest.
Arguments:
- record: bfloat16 [2048, 12288], P(('groups', 'chan')), parts along dimension 0, may hold values from -2000 to 2000
- starts: int32 [4], P('groups'), parts along dimension 0, may hold values from 0 to 8192, as said below
- send_rows: int32 [32, 16, 2], P(('groups', 'chan')), parts along dimension 0, may hold values from 0 to 63, as said below
- send_count: int32 [32, 16], P(('groups', 'chan')), parts along dimension 0, may hold values from 0 to 2, as said below
- pair_slots: int32 [2, 16384], P(None, ('groups', 'chan')), parts along dimension 1, may hold values from -1 to 31, as said below
- pair_count: int32 [32], P(('groups', 'chan')), parts along dimension 0, may hold values from 1 to 512, as said below
Outputs:
- correlations: float32 [16384, 512], P(('groups', 'chan')), parts along dimension 0
The draws below stay inside these ranges and needn't reach their ends.
There are 2 independent parts, one for each index of `groups`. The reference program is written for one: setup_inputs(seed, part) draws one part's arguments, and reference() takes and returns one part's arrays. A program takes and returns all parts, laid end to end along the dimension named above; each array names one. Nothing has to cross between parts.
Inputs may be any that keep to these rules, and one draw needn't show every extreme that they name: Window starts never fall. `send_rows`: local channel numbers; the slots of one device to one owner name distinct channels. `send_count`: some owner receives 2 rows from every device; every device sends at least one row to itself as owner. `pair_count`: each owner has at least as many live pairs as it receives live rows; some owner has 512. `pair_slots`: a live pair names two live slots of its owner, distinct where the owner has two or more live slots; every live slot is named by some pair; entries of pairs at or beyond pair_count are -1.
All inputs are finite; a program needn't handle non-finite values.
Results may differ from the reference program's by a relative error of at most 0.0059.
Values may be sent and summed in bfloat16 or wider, within the bound.
A program may use at most 192 MiB of HBM per device.

```python
import math
import jax
import jax.numpy as jnp
from jax import lax

F = 2048
WLEN = 4096
BAND = 64
LAGS = 512
CAP = 2
CH_DEV = 64
NWIN = 2
PAIR_CAP = 512
CHANNELS = 1024
SAMPLES = 12288
N_CHAN = 16


def draw_record(key, part):
    keys = jax.random.split(key, 6)
    samples = jnp.arange(SAMPLES, dtype=jnp.float32)
    position = jnp.arange(CHANNELS, dtype=jnp.float32)[:, None] / CHANNELS
    ramp = 1.0 + 2.0 * position
    noise = jax.random.truncated_normal(keys[0], -5.0, 5.0, (CHANNELS, SAMPLES), jnp.float32)
    gains = jnp.exp(jax.random.uniform(keys[1], (CHANNELS, 1), jnp.float32, 0.0, math.log(10.0)))
    amps = jnp.exp(jax.random.uniform(keys[2], (4,), jnp.float32, 0.0, math.log(6.0)))
    common_scale = 2.0
    freqs = jax.random.uniform(keys[3], (4,), jnp.float32, 0.02, 0.45)
    phases = jax.random.uniform(keys[4], (CHANNELS, 4), jnp.float32, -math.pi, math.pi)
    tones = jnp.zeros((CHANNELS, SAMPLES), jnp.float32)
    for tone_idx in range(4):
        cycle = jnp.mod(freqs[tone_idx] * samples, 1.0)[None, :]
        tones = tones + amps[tone_idx] * jnp.cos(2.0 * math.pi * cycle + phases[:, tone_idx:tone_idx + 1])
    common = jax.random.truncated_normal(keys[5], -5.0, 5.0, (1, SAMPLES), jnp.float32) * common_scale
    values = gains * ramp * (noise + tones) + common
    return values.astype(jnp.bfloat16)


def draw_starts(key, part):
    jitter = jax.random.randint(jax.random.fold_in(key, 3), (NWIN,), 0, WLEN + 1)
    window_ids = jnp.arange(NWIN, dtype=jnp.int32)
    firsts = window_ids * WLEN + jitter
    firsts = jnp.where(window_ids == NWIN - 1, NWIN * WLEN, firsts)
    return firsts.astype(jnp.int32)


def routing(key):
    base = jax.random.fold_in(key, 11)
    key_a, key_b, key_c, key_d, key_e, key_f = jax.random.split(base, 6)
    owners = jnp.arange(N_CHAN, dtype=jnp.int32)
    counts = jax.random.randint(key_a, (N_CHAN, N_CHAN), 0, CAP + 1)
    full_owner = jax.random.randint(key_b, (), 0, N_CHAN)
    counts = jnp.where(owners[:, None] == full_owner, CAP, counts)
    counts = jnp.where(owners[:, None] == owners[None, :], jnp.maximum(counts, 1), counts)
    scores = jax.random.randint(key_c, (N_CHAN, N_CHAN, CH_DEV), 0, 2 ** 20) * CH_DEV + jnp.arange(CH_DEV, dtype=jnp.int32)
    picks = jnp.argsort(scores, axis=-1)[..., :CAP].astype(jnp.int32)
    slot_total = N_CHAN * CAP
    slot_ids = jnp.arange(slot_total, dtype=jnp.int32)
    source = slot_ids // CAP
    within = slot_ids % CAP
    live = within[None, :] < counts[:, source]
    live_total = jnp.sum(live.astype(jnp.int32), axis=1)
    order = jnp.argsort(jnp.where(live, slot_ids[None, :], slot_ids[None, :] + slot_total), axis=1).astype(jnp.int32)
    spread = jax.random.randint(key_d, (N_CHAN,), 0, 8)
    pair_num = jnp.minimum(live_total + live_total * spread * spread // 16, PAIR_CAP)
    busy = jax.random.randint(key_e, (), 0, N_CHAN)
    pair_num = jnp.where(owners == busy, PAIR_CAP, pair_num).astype(jnp.int32)
    pair_idx = jnp.arange(PAIR_CAP, dtype=jnp.int32)
    first_pos = pair_idx[None, :] % live_total[:, None]
    jumps = jax.random.randint(key_f, (N_CHAN, PAIR_CAP), 0, 2 ** 20) % jnp.maximum(live_total - 1, 1)[:, None]
    second_pos = (first_pos + 1 + jumps) % live_total[:, None]
    first_slot = jnp.take_along_axis(order, first_pos, axis=1)
    second_slot = jnp.take_along_axis(order, second_pos, axis=1)
    alive = pair_idx[None, :] < pair_num[:, None]
    first_slot = jnp.where(alive, first_slot, -1)
    second_slot = jnp.where(alive, second_slot, -1)
    slots = jnp.stack([first_slot.reshape(-1), second_slot.reshape(-1)], axis=0).astype(jnp.int32)
    return (counts.astype(jnp.int32), picks, pair_num, slots)


def draw_send_rows(key, part):
    counts, picks, pair_num, slots = routing(key)
    return picks.transpose(1, 0, 2).astype(jnp.int32)


def draw_send_count(key, part):
    counts, picks, pair_num, slots = routing(key)
    return counts.T.astype(jnp.int32)


def draw_pair_slots(key, part):
    counts, picks, pair_num, slots = routing(key)
    return slots


def draw_pair_count(key, part):
    counts, picks, pair_num, slots = routing(key)
    return pair_num


def setup_inputs(seed: int = 0, part: int = 0) -> dict:
    key_list = jax.random.split(jax.random.key(seed), 7)
    part_splits = jax.random.split(jax.random.fold_in(key_list[6], part), 7)
    record = draw_record(jax.random.fold_in(jax.random.fold_in(key_list[6], part), 71), part)
    starts = draw_starts(jax.random.fold_in(jax.random.fold_in(key_list[6], part), 71), part)
    send_rows = draw_send_rows(jax.random.fold_in(jax.random.fold_in(key_list[6], part), 71), part)
    send_count = draw_send_count(jax.random.fold_in(jax.random.fold_in(key_list[6], part), 71), part)
    pair_slots = draw_pair_slots(jax.random.fold_in(jax.random.fold_in(key_list[6], part), 71), part)
    pair_count = draw_pair_count(jax.random.fold_in(jax.random.fold_in(key_list[6], part), 71), part)
    return dict(record=record, starts=starts, send_rows=send_rows, send_count=send_count, pair_slots=pair_slots, pair_count=pair_count)


def taper_window():
    samples = jnp.arange(WLEN, dtype=jnp.float32)
    return 0.5 - 0.5 * jnp.cos(2.0 * math.pi / WLEN * samples)

def dft_block(first_bin, width):
    sample_idx = jnp.arange(WLEN, dtype=jnp.int32)[:, None]
    bin_idx = first_bin + jnp.arange(width, dtype=jnp.int32)[None, :]
    phases = (sample_idx * bin_idx % WLEN).astype(jnp.float32) * (2.0 * math.pi / WLEN)
    return (jnp.cos(phases).astype(jnp.bfloat16), (-jnp.sin(phases)).astype(jnp.bfloat16))

def lag_table():
    bin_idx = jnp.arange(F, dtype=jnp.int32)[:, None]
    shifts = (jnp.arange(LAGS, dtype=jnp.int32) - LAGS // 2) % WLEN
    phases = (bin_idx * shifts[None, :] % WLEN).astype(jnp.float32) * (2.0 * math.pi / WLEN)
    factor = 1.0 / math.sqrt(F)
    return jnp.concatenate([jnp.cos(phases) * factor, -jnp.sin(phases) * factor], axis=0).astype(jnp.bfloat16)

def whiten(real_part, imag_part):
    leading = real_part.shape[:-1]
    bands = F // BAND
    powers = real_part * real_part + imag_part * imag_part
    band_power = powers.reshape(leading + (bands, BAND)).sum(-1) / (2.0 * BAND)
    scales = (1.0 / jnp.sqrt(band_power + 1e-06))[..., None]
    real_white = (real_part.reshape(leading + (bands, BAND)) * scales).reshape(leading + (F,))
    imag_white = (imag_part.reshape(leading + (bands, BAND)) * scales).reshape(leading + (F,))
    return jnp.concatenate([real_white, imag_white], axis=-1).astype(jnp.bfloat16)

def windows_of(record, starts):
    taper_win = taper_window()
    pieces = jax.vmap(lambda offset: lax.dynamic_slice_in_dim(record, offset, WLEN, 1))(starts)
    return (pieces.astype(jnp.float32) * taper_win).astype(jnp.bfloat16)

def reference(record, starts, send_rows, send_count, pair_slots, pair_count):
    segments = windows_of(record, starts)
    flat_rows = segments.reshape(NWIN * CHANNELS, WLEN)
    cos_tab, sin_tab = dft_block(0, F)
    real_part = jnp.dot(flat_rows, cos_tab, preferred_element_type=jnp.float32).reshape(NWIN, CHANNELS, F)
    imag_part = jnp.dot(flat_rows, sin_tab, preferred_element_type=jnp.float32).reshape(NWIN, CHANNELS, F)
    real_part = real_part - lax.optimization_barrier(jnp.sum(real_part, axis=1, keepdims=True)) / CHANNELS
    imag_part = imag_part - lax.optimization_barrier(jnp.sum(imag_part, axis=1, keepdims=True)) / CHANNELS
    whitened = whiten(real_part, imag_part)
    bases = (jnp.arange(N_CHAN, dtype=jnp.int32) * CH_DEV)[None, :, None]
    slot_chan = (send_rows.transpose(1, 0, 2) + bases).reshape(N_CHAN, N_CHAN * CAP)
    slot_alive = (jnp.arange(CAP, dtype=jnp.int32)[None, None, :] < send_count.T[:, :, None]).reshape(N_CHAN, N_CHAN * CAP)
    lag_tab = lag_table()
    slots_by_owner = pair_slots.reshape(2, N_CHAN, PAIR_CAP).transpose(1, 0, 2)

    def owner_work(inputs):
        slot_chans, slot_live, pair_list, live_pairs = inputs

        def rows_of(member):
            slot_idx = jnp.maximum(pair_list[member], 0)
            picked = jnp.take(whitened, jnp.take(slot_chans, slot_idx), axis=1)
            keep = jnp.take(slot_live, slot_idx)[None, :, None]
            return jnp.where(keep, picked, jnp.zeros_like(picked)).astype(jnp.float32)
        first_rows = rows_of(0)
        second = rows_of(1)
        real_a, imag_a = (first_rows[..., :F], first_rows[..., F:])
        real_b, imag_b = (second[..., :F], second[..., F:])
        cross_real = lax.optimization_barrier(jnp.sum(real_a * real_b + imag_a * imag_b, axis=0)) / NWIN
        cross_imag = lax.optimization_barrier(jnp.sum(imag_a * real_b - real_a * imag_b, axis=0)) / NWIN
        cross_spec = jnp.concatenate([cross_real, cross_imag], axis=1).astype(jnp.bfloat16)
        lagged = jnp.dot(cross_spec, lag_tab, preferred_element_type=jnp.float32)
        is_alive = jnp.arange(PAIR_CAP, dtype=jnp.int32) < live_pairs
        return jnp.where(is_alive[:, None], lagged, jnp.zeros_like(lagged))
    result = lax.map(owner_work, (slot_chan, slot_alive, slots_by_owner, pair_count))
    return result.reshape(N_CHAN * PAIR_CAP, LAGS)
```

```python
import functools
import math

import jax
import jax.numpy as jnp
import numpy as np
from jax import lax
from jax.experimental import pallas as pl
from jax.experimental.pallas import tpu as pltpu
from jax.sharding import PartitionSpec as P

F = 2048
WLEN = 4096
BAND = 64
LAGS = 512
RAD = 16
T2 = WLEN // RAD
F2 = F // RAD
BLK = 2 * T2
VMEM_LIMIT = 56 * 2**20
MESH = pl.DeviceIdType.MESH


def tables():
    t2 = np.arange(T2)[:, None]
    f2 = np.arange(F2)[None, :]

    def trig(f1):
        angle = 2.0 * np.pi * ((t2 * (RAD * f2 + f1)) % WLEN) / WLEN
        return np.cos(angle), np.sin(angle)

    groups = []
    zero = np.zeros((T2, 2 * F2))
    cos0, sin0 = trig(0)
    cos8, sin8 = trig(RAD // 2)
    top = np.concatenate([cos0, -sin0, zero], 1)
    low = np.concatenate([zero, cos8, -sin8], 1)
    groups.append(np.concatenate([top, low], 0))
    for g in range(1, RAD // 2):
        cos_a, sin_a = trig(g)
        cos_b, sin_b = trig(RAD - g)
        top = np.concatenate([cos_a, -sin_a, cos_b, -sin_b], 1)
        low = np.concatenate([sin_a, cos_a, -sin_b, -cos_b], 1)
        groups.append(np.concatenate([top, low], 0))
    dft = np.stack(groups).astype(jnp.bfloat16)

    shifts = (np.arange(LAGS) - LAGS // 2) % WLEN
    lag = []
    for g in range(RAD // 2):
        for f1 in (g, RAD - g if g else RAD // 2):
            f = (RAD * np.arange(F2) + f1)[:, None]
            angle = 2.0 * np.pi * ((f * shifts[None, :]) % WLEN) / WLEN
            lag.append(np.cos(angle) / math.sqrt(F))
            lag.append(-np.sin(angle) / math.sqrt(F))
    lag = np.concatenate(lag, 0).astype(jnp.bfloat16)

    taper = 0.5 - 0.5 * np.cos(2.0 * np.pi * np.arange(WLEN) / WLEN)
    return dft, lag, taper.astype(np.float32).reshape(RAD, T2)


def cut_windows(rec_ref, starts_ref, win_ref):
    lane = lax.broadcasted_iota(jnp.int32, (rec_ref.shape[0], 128), 1)
    last = rec_ref.shape[1] - 128
    for w in range(win_ref.shape[0]):
        first = starts_ref[w]
        shift = first % 128
        base = first - shift

        def turned(m):
            at = pl.multiple_of(jnp.minimum(base + m * 128, last), 128)
            piece = rec_ref[:, pl.ds(at, 128)].astype(jnp.float32)
            return pltpu.roll(piece, (128 - shift) % 128, 1)

        here = turned(0)
        for m in range(WLEN // 128):
            after = turned(m + 1)
            win_ref[w, :, m * 128 : (m + 1) * 128] = jnp.where(lane < 128 - shift, here, after)
            here = after


def sum_channels(win_ref, part_ref):
    for w in range(win_ref.shape[0]):
        for j in range(RAD):
            total = jnp.sum(win_ref[w, :, j * T2 : (j + 1) * T2], axis=0, keepdims=True)
            part_ref[j, :, w * T2 : (w + 1) * T2] = total


def column(row):
    n = row.shape[1]
    down = lax.broadcasted_iota(jnp.int32, (n, n), 0)
    across = lax.broadcasted_iota(jnp.int32, (n, n), 1)
    return jnp.sum(jnp.where(down == across, row, 0.0), axis=1, keepdims=True)


def pick_rows(n, win_ref, rows_ref, count_ref, wide_ref, out_ref):
    chans = win_ref.shape[1]
    caps = rows_ref.shape[0]
    lane = lax.broadcasted_iota(jnp.int32, (n, chans), 1).astype(jnp.float32)
    for k in range(caps):
        picks = jnp.where(count_ref[...] > k, rows_ref[k : k + 1, :], -1).astype(jnp.float32)
        hot = jnp.where(lane == column(picks), 1.0, 0.0).astype(jnp.bfloat16)
        for w in range(2):
            for j in range(RAD):
                picked = jnp.dot(
                    hot,
                    win_ref[w, :, j * T2 : (j + 1) * T2].astype(jnp.bfloat16),
                    preferred_element_type=jnp.float32,
                )
                for half in range(2):
                    c = (k * 2 + w) * 2 + half
                    wide_ref[c, pl.ds(j, n, stride=RAD), :] = picked[:, half * 128 : (half + 1) * 128]
    for c in range(4 * caps):
        block = wide_ref[c].reshape(n, RAD, 128).astype(jnp.bfloat16)
        out_ref[c // 4, :, :, (c % 4) * 128 : (c % 4 + 1) * 128] = block


def cut_kernel(n, split, rec_ref, starts_ref, rows_ref, count_ref, out_ref, part_ref, win, wide, slab):
    cut_windows(rec_ref, starts_ref, win)
    if split == 1:
        sum_channels(win, part_ref)
    else:
        sum_channels(win, slab)
        width = slab.shape[2] // split
        for i in range(n):
            lo = (i % split) * width
            part_ref[i] = slab[i // split][:, lo : lo + width]
    pick_rows(n, win, rows_ref, count_ref, wide, out_ref)


def exchange_kernel(
    n, split, chans, outgoing, part, taper_ref, dft_hbm, white_ref,
    incoming, parts, total, slab, wide, lhs, spec, dft,
    row_send, row_recv, part_send, part_recv, sum_send, sum_recv, local_sem, dft_sem,
):
    me = lax.axis_index("chan")
    caps = outgoing.shape[0]
    dft_copy = pltpu.make_async_copy(dft_hbm, dft, dft_sem)
    dft_copy.start()

    def peer(d):
        return lax.rem(me + d, n)

    def remote(src, dst, send, recv, d):
        return pltpu.make_async_remote_copy(
            src_ref=src, dst_ref=dst, send_sem=send, recv_sem=recv,
            device_id={"chan": peer(d)}, device_id_type=MESH,
        )

    def row_copy(k, d):
        at = k * n + d
        return remote(outgoing.at[k, peer(d)], incoming.at[k, me], row_send.at[at], row_recv.at[at], d)

    def part_copy(d):
        return remote(part.at[peer(d)], parts.at[me], part_send.at[d], part_recv.at[d], d)

    def sum_copy(d):
        return remote(total.at[me], total.at[me], sum_send.at[d], sum_recv.at[d], d)

    def each(fn):
        def step(i, carry):
            fn(n // 2 + (2 * (i % 2) - 1) * ((i + 1) // 2))
            return carry

        lax.fori_loop(0, n - 1, step, 0)

    barrier = pltpu.get_barrier_semaphore()
    each(lambda d: pl.semaphore_signal(barrier, inc=1, device_id={"chan": peer(d)}, device_id_type=MESH))
    pl.semaphore_wait(barrier, n - 1)
    each(lambda d: part_copy(d).start())
    each(lambda d: row_copy(0, d).start())
    own = [pltpu.make_async_copy(outgoing.at[k, me], incoming.at[k, me], local_sem.at[k]) for k in range(caps)]
    for copy in own:
        copy.start()
    parts[me] = part[me]
    each(lambda d: part_copy(d).wait_recv())
    total[me] = jnp.sum(parts[...], axis=0)
    each(lambda d: sum_copy(d).start())
    for k in range(1, caps):
        each(functools.partial(lambda k, d: row_copy(k, d).start(), k))
    for copy in own:
        copy.wait()
    each(lambda d: sum_copy(d).wait_recv())
    width = slab.shape[2] // split
    for i in range(n):
        lo = (i % split) * width
        slab[i // split, :, lo : lo + width] = total[i] * (1.0 / chans)
    for k in range(caps):
        each(functools.partial(lambda k, d: row_copy(k, d).wait_recv(), k))
        short_dfts(n, k, incoming, slab, taper_ref, wide, lhs)
    dft_copy.wait()
    whiten(n, caps, lhs, dft, spec, white_ref)
    each(lambda d: part_copy(d).wait_send())
    each(lambda d: sum_copy(d).wait_send())
    for k in range(caps):
        each(functools.partial(lambda k, d: row_copy(k, d).wait_send(), k))


def real_dft(xs):
    size = len(xs)
    if size == 1:
        return [(xs[0], None)]
    even, odd = real_dft(xs[0::2]), real_dft(xs[1::2])
    if size == 2:
        return [(even[0][0] + odd[0][0], None), (even[0][0] - odd[0][0], None)]
    out = [None] * (size // 2 + 1)
    for k in range(size // 4 + 1):
        (er, ei), (or_, oi) = even[k], odd[k]
        c, s = math.cos(2 * math.pi * k / size), math.sin(2 * math.pi * k / size)
        if k == 0:
            tr, ti = or_, None
        elif 4 * k == size:
            tr, ti = oi, -or_
        elif oi is None:
            tr, ti = c * or_, -s * or_
        else:
            tr, ti = c * or_ + s * oi, c * oi - s * or_

        def plus(a, b):
            return b if a is None else a if b is None else a + b

        def minus(a, b):
            if b is None:
                return a
            return -b if a is None else a - b

        out[k] = (plus(er, tr), plus(ei, ti))
        if 4 * k == size:
            continue
        low = minus(ei, ti)
        out[size // 2 - k] = (minus(er, tr), None if low is None else -low)
    return out


def short_dfts(n, k, incoming, mean_ref, taper_ref, wide, lhs):
    for c in range(4):
        wide[k * 4 + c] = incoming[k, :, :, c * 128 : (c + 1) * 128].astype(jnp.float32).reshape(n * RAD, 128)
    for c in range(4):
        w, half = c // 2, c % 2
        cols = slice(half * 128, (half + 1) * 128)
        xs = []
        for j in range(RAD):
            mean = mean_ref[j, :, c * 128 : (c + 1) * 128]
            xs.append((wide[k * 4 + c, pl.ds(j, n, stride=RAD), :] - mean) * taper_ref[j : j + 1, cols])
        bins = real_dft(xs)
        rows = slice((k * 2 + w) * n, (k * 2 + w + 1) * n)
        right = slice(T2 + half * 128, T2 + (half + 1) * 128)
        lhs[0, rows, cols] = bins[0][0].astype(jnp.bfloat16)
        lhs[0, rows, right] = bins[RAD // 2][0].astype(jnp.bfloat16)
        for g in range(1, RAD // 2):
            lhs[g, rows, cols] = bins[g][0].astype(jnp.bfloat16)
            lhs[g, rows, right] = bins[g][1].astype(jnp.bfloat16)


def whiten(n, caps, lhs, dft_ref, spec, white):
    power = jnp.zeros((lhs.shape[1], F2), jnp.float32)
    for g in range(RAD // 2):
        block = jnp.dot(lhs[g], dft_ref[g], preferred_element_type=jnp.float32)
        spec[g] = block
        for q in range(4):
            piece = block[:, q * F2 : (q + 1) * F2]
            power = power + piece * piece
    lane = lax.broadcasted_iota(jnp.int32, power.shape, 1)
    for step in (1, 2):
        low = (lane // step) % 2 == 0
        power = power + jnp.where(low, pltpu.roll(power, F2 - step, 1), pltpu.roll(power, step, 1))
    scale = 1.0 / jnp.sqrt(power * (1.0 / (2 * BAND)) + 1e-06)
    for g in range(RAD // 2):
        for q in range(4):
            piece = (spec[g, :, q * F2 : (q + 1) * F2] * scale).astype(jnp.bfloat16)
            at = g * BLK + q * F2
            for kw in range(2 * caps):
                k, w = kw // 2, kw % 2
                white[w, k * n : (k + 1) * n, at : at + F2] = piece[kw * n : (kw + 1) * n]


def pairs_kernel(n, white, pairs_ref, live_ref, lag_hbm, out_ref, cross, lag, lag_sem):
    lag_copy = pltpu.make_async_copy(lag_hbm, lag, lag_sem)
    lag_copy.start()
    caps = white.shape[1] // n
    wide = max(128, caps * n)
    pair_cap = pairs_ref.shape[1]
    row = lax.broadcasted_iota(jnp.int32, (wide, pair_cap), 0)
    slot = jnp.where(row < caps * n, (row % n) * caps + row // n, caps * n)
    alive = lax.broadcasted_iota(jnp.int32, (1, pair_cap), 1) < live_ref[0]
    hots = []
    for member in range(2):
        index = jnp.where(alive, pairs_ref[member : member + 1, :], -1)
        hot = jnp.where(slot == index, 1.0, 0.0).T
        hots.append(hot[:, : caps * n].astype(jnp.bfloat16))
    chunk = 256
    for lo in range(0, pair_cap, chunk):
        hot_a, hot_b = hots[0][lo : lo + chunk], hots[1][lo : lo + chunk]
        for block in range(RAD):
            cols = slice(block * T2, (block + 1) * T2)
            real = imag = 0.0
            for w in range(2):
                a = jnp.dot(hot_a, white[w, :, cols], preferred_element_type=jnp.float32)
                b = jnp.dot(hot_b, white[w, :, cols], preferred_element_type=jnp.float32)
                ra, ia, rb, ib = a[:, :F2], a[:, F2:], b[:, :F2], b[:, F2:]
                real = real + (ra * rb + ia * ib)
                imag = imag + (ia * rb - ra * ib)
            cross[lo // chunk, :, block * T2 : block * T2 + F2] = (real * 0.5).astype(jnp.bfloat16)
            cross[lo // chunk, :, block * T2 + F2 : (block + 1) * T2] = (imag * 0.5).astype(jnp.bfloat16)
        if lo == 0:
            lag_copy.wait()
        out_ref[lo : lo + chunk, :] = jnp.dot(cross[lo // chunk], lag[...], preferred_element_type=jnp.float32)


def body(record, starts, send_rows, send_count, pair_slots, pair_count):
    local, windows = record.shape[0], starts.shape[0]
    n, caps = send_rows.shape[1], send_rows.shape[2]
    lanes = caps * windows * T2
    split = n // RAD
    width = windows * WLEN // n
    pair_cap = pair_slots.shape[1]
    f32, bf16 = jnp.float32, jnp.bfloat16
    vmem, smem = pl.BlockSpec(memory_space=pltpu.VMEM), pl.BlockSpec(memory_space=pltpu.SMEM)
    dma = pltpu.SemaphoreType.DMA
    hbm = pl.BlockSpec(memory_space=pl.ANY)
    rows_shape = (caps, n, RAD, windows * T2)
    part_shape = (n, 1, width)
    slab_shape = (RAD, 1, windows * T2)
    outgoing, part = pl.pallas_call(
        functools.partial(cut_kernel, n, split),
        out_shape=(jax.ShapeDtypeStruct(rows_shape, bf16), jax.ShapeDtypeStruct(part_shape, f32)),
        in_specs=[vmem, smem, vmem, vmem],
        out_specs=(vmem, vmem),
        scratch_shapes=[
            pltpu.VMEM((windows, local, WLEN), f32),
            pltpu.VMEM((lanes // 128, n * RAD, 128), f32),
            pltpu.VMEM(slab_shape, f32),
        ],
        compiler_params=pltpu.CompilerParams(vmem_limit_bytes=VMEM_LIMIT),
        name="cut",
    )(record, starts, send_rows[0].T, send_count)
    dft, lag, taper = tables()
    rows = caps * windows * n
    white = pl.pallas_call(
        functools.partial(exchange_kernel, n, split, local * n),
        out_shape=jax.ShapeDtypeStruct((windows, caps * n, 2 * F), bf16),
        in_specs=[vmem, vmem, vmem, hbm],
        out_specs=vmem,
        scratch_shapes=[
            pltpu.VMEM(rows_shape, bf16),
            pltpu.VMEM(part_shape, f32),
            pltpu.VMEM(part_shape, f32),
            pltpu.VMEM(slab_shape, f32),
            pltpu.VMEM((lanes // 128, n * RAD, 128), f32),
            pltpu.VMEM((RAD // 2, rows, BLK), bf16),
            pltpu.VMEM((RAD // 2, rows, BLK), f32),
            pltpu.VMEM(dft.shape, bf16),
            dma((caps * n,)), dma((caps * n,)), dma((n,)), dma((n,)), dma((n,)), dma((n,)), dma((caps,)), dma,
        ],
        compiler_params=pltpu.CompilerParams(
            collective_id=0, has_side_effects=True, vmem_limit_bytes=VMEM_LIMIT
        ),
        name="exchange",
    )(outgoing, part, jnp.asarray(taper), jnp.asarray(dft))
    return pl.pallas_call(
        functools.partial(pairs_kernel, n),
        out_shape=jax.ShapeDtypeStruct((pair_cap, LAGS), f32),
        in_specs=[vmem, vmem, smem, hbm],
        out_specs=vmem,
        scratch_shapes=[
            pltpu.VMEM((pair_cap // 256, 256, 2 * F), bf16),
            pltpu.VMEM(lag.shape, bf16),
            dma,
        ],
        compiler_params=pltpu.CompilerParams(vmem_limit_bytes=VMEM_LIMIT),
        name="pairs",
    )(white, pair_slots, pair_count, jnp.asarray(lag))


def solution(mesh):
    in_specs = (
        P(("groups", "chan"), None),
        P("groups"),
        P(("groups", "chan"), None, None),
        P(("groups", "chan"), None),
        P(None, ("groups", "chan")),
        P(("groups", "chan")),
    )
    out_specs = P(("groups", "chan"), None)
    return jax.shard_map(body, mesh=mesh, in_specs=in_specs, out_specs=out_specs, check_vma=False)
```

```python
import functools
import math

import jax
import jax.numpy as jnp
import numpy as np
from jax import lax
from jax.experimental import pallas as pl
from jax.experimental.pallas import tpu as pltpu
from jax.sharding import PartitionSpec as P

F = 2048
WLEN = 4096
BAND = 64
LAGS = 512
RAD = 16
T2 = WLEN // RAD
F2 = F // RAD
BLK = 2 * T2
VMEM_LIMIT = 56 * 2**20
MESH = pl.DeviceIdType.MESH


def tables():
    t2 = np.arange(T2)[:, None]
    f2 = np.arange(F2)[None, :]

    def trig(f1):
        angle = 2.0 * np.pi * ((t2 * (RAD * f2 + f1)) % WLEN) / WLEN
        return np.cos(angle), np.sin(angle)

    groups = []
    zero = np.zeros((T2, 2 * F2))
    cos0, sin0 = trig(0)
    cos8, sin8 = trig(RAD // 2)
    top = np.concatenate([cos0, -sin0, zero], 1)
    low = np.concatenate([zero, cos8, -sin8], 1)
    groups.append(np.concatenate([top, low], 0))
    for g in range(1, RAD // 2):
        cos_a, sin_a = trig(g)
        cos_b, sin_b = trig(RAD - g)
        top = np.concatenate([cos_a, -sin_a, cos_b, -sin_b], 1)
        low = np.concatenate([sin_a, cos_a, -sin_b, -cos_b], 1)
        groups.append(np.concatenate([top, low], 0))
    dft = np.stack(groups).astype(jnp.bfloat16)

    shifts = (np.arange(LAGS) - LAGS // 2) % WLEN
    lag = []
    for g in range(RAD // 2):
        for f1 in (g, RAD - g if g else RAD // 2):
            f = (RAD * np.arange(F2) + f1)[:, None]
            angle = 2.0 * np.pi * ((f * shifts[None, :]) % WLEN) / WLEN
            lag.append(np.cos(angle) / math.sqrt(F))
            lag.append(-np.sin(angle) / math.sqrt(F))
    lag = np.concatenate(lag, 0).astype(jnp.bfloat16)

    taper = 0.5 - 0.5 * np.cos(2.0 * np.pi * np.arange(WLEN) / WLEN)
    return dft, lag, taper.astype(np.float32).reshape(RAD, T2)


def cut_windows(rec_ref, starts_ref, win_ref):
    lane = lax.broadcasted_iota(jnp.int32, (rec_ref.shape[0], 128), 1)
    last = rec_ref.shape[1] - 128
    for w in range(win_ref.shape[0]):
        first = starts_ref[w]
        shift = first % 128
        base = first - shift

        def turned(m):
            at = pl.multiple_of(jnp.minimum(base + m * 128, last), 128)
            piece = rec_ref[:, pl.ds(at, 128)].astype(jnp.float32)
            return pltpu.roll(piece, (128 - shift) % 128, 1)

        here = turned(0)
        for m in range(WLEN // 128):
            after = turned(m + 1)
            win_ref[w, :, m * 128 : (m + 1) * 128] = jnp.where(lane < 128 - shift, here, after)
            here = after


def sum_channels(win_ref, part_ref):
    for w in range(win_ref.shape[0]):
        for j in range(RAD):
            total = jnp.sum(win_ref[w, :, j * T2 : (j + 1) * T2], axis=0, keepdims=True)
            part_ref[j, :, w * T2 : (w + 1) * T2] = total


def column(row):
    n = row.shape[1]
    down = lax.broadcasted_iota(jnp.int32, (n, n), 0)
    across = lax.broadcasted_iota(jnp.int32, (n, n), 1)
    return jnp.sum(jnp.where(down == across, row, 0.0), axis=1, keepdims=True)


def pick_rows(n, win_ref, rows_ref, count_ref, wide_ref, out_ref):
    chans = win_ref.shape[1]
    caps = rows_ref.shape[0]
    lane = lax.broadcasted_iota(jnp.int32, (n, chans), 1).astype(jnp.float32)
    for k in range(caps):
        picks = jnp.where(count_ref[...] > k, rows_ref[k : k + 1, :], -1).astype(jnp.float32)
        hot = jnp.where(lane == column(picks), 1.0, 0.0).astype(jnp.bfloat16)
        for w in range(2):
            for j in range(RAD):
                picked = jnp.dot(
                    hot,
                    win_ref[w, :, j * T2 : (j + 1) * T2].astype(jnp.bfloat16),
                    preferred_element_type=jnp.float32,
                )
                for half in range(2):
                    c = (k * 2 + w) * 2 + half
                    wide_ref[c, pl.ds(j, n, stride=RAD), :] = picked[:, half * 128 : (half + 1) * 128]
    for c in range(4 * caps):
        block = wide_ref[c].reshape(n, RAD, 128).astype(jnp.bfloat16)
        out_ref[c // 4, :, :, (c % 4) * 128 : (c % 4 + 1) * 128] = block


def cut_kernel(n, split, rec_ref, starts_ref, rows_ref, count_ref, out_ref, part_ref, win, wide, slab):
    cut_windows(rec_ref, starts_ref, win)
    if split == 1:
        sum_channels(win, part_ref)
    else:
        sum_channels(win, slab)
        width = slab.shape[2] // split
        for i in range(n):
            lo = (i % split) * width
            part_ref[i] = slab[i // split][:, lo : lo + width]
    pick_rows(n, win, rows_ref, count_ref, wide, out_ref)


def exchange_kernel(
    n, split, chans, outgoing, part, taper_ref, dft_hbm, white_ref,
    incoming, parts, total, slab, wide, lhs, spec, dft,
    row_send, row_recv, part_send, part_recv, sum_send, sum_recv, local_sem, dft_sem,
):
    me = lax.axis_index("chan")
    caps = outgoing.shape[0]
    dft_copy = pltpu.make_async_copy(dft_hbm, dft, dft_sem)
    dft_copy.start()

    def peer(d):
        return lax.rem(me + d, n)

    def remote(src, dst, send, recv, d):
        return pltpu.make_async_remote_copy(
            src_ref=src, dst_ref=dst, send_sem=send, recv_sem=recv,
            device_id={"chan": peer(d)}, device_id_type=MESH,
        )

    def row_copy(k, d):
        at = k * n + d
        return remote(outgoing.at[k, peer(d)], incoming.at[k, me], row_send.at[at], row_recv.at[at], d)

    def part_copy(d):
        return remote(part.at[peer(d)], parts.at[me], part_send.at[d], part_recv.at[d], d)

    def sum_copy(d):
        return remote(total.at[me], total.at[me], sum_send.at[d], sum_recv.at[d], d)

    def each(fn):
        def step(i, carry):
            fn(n // 2 + (2 * (i % 2) - 1) * ((i + 1) // 2))
            return carry

        lax.fori_loop(0, n - 1, step, 0)

    barrier = pltpu.get_barrier_semaphore()
    each(lambda d: pl.semaphore_signal(barrier, inc=1, device_id={"chan": peer(d)}, device_id_type=MESH))
    pl.semaphore_wait(barrier, n - 1)
    each(lambda d: part_copy(d).start())
    each(lambda d: row_copy(0, d).start())
    own = [pltpu.make_async_copy(outgoing.at[k, me], incoming.at[k, me], local_sem.at[k]) for k in range(caps)]
    for copy in own:
        copy.start()
    parts[me] = part[me]
    each(lambda d: part_copy(d).wait_recv())
    total[me] = jnp.sum(parts[...], axis=0)
    each(lambda d: sum_copy(d).start())
    for k in range(1, caps):
        each(functools.partial(lambda k, d: row_copy(k, d).start(), k))
    for copy in own:
        copy.wait()
    each(lambda d: sum_copy(d).wait_recv())
    width = slab.shape[2] // split
    for i in range(n):
        lo = (i % split) * width
        slab[i // split, :, lo : lo + width] = total[i] * (1.0 / chans)
    for k in range(caps):
        each(functools.partial(lambda k, d: row_copy(k, d).wait_recv(), k))
        short_dfts(n, k, incoming, slab, taper_ref, wide, lhs)
    dft_copy.wait()
    whiten(n, caps, lhs, dft, spec, white_ref)
    each(lambda d: part_copy(d).wait_send())
    each(lambda d: sum_copy(d).wait_send())
    for k in range(caps):
        each(functools.partial(lambda k, d: row_copy(k, d).wait_send(), k))


def real_dft(xs):
    size = len(xs)
    if size == 1:
        return [(xs[0], None)]
    even, odd = real_dft(xs[0::2]), real_dft(xs[1::2])
    if size == 2:
        return [(even[0][0] + odd[0][0], None), (even[0][0] - odd[0][0], None)]
    out = [None] * (size // 2 + 1)
    for k in range(size // 4 + 1):
        (er, ei), (or_, oi) = even[k], odd[k]
        c, s = math.cos(2 * math.pi * k / size), math.sin(2 * math.pi * k / size)
        if k == 0:
            tr, ti = or_, None
        elif 4 * k == size:
            tr, ti = oi, -or_
        elif oi is None:
            tr, ti = c * or_, -s * or_
        else:
            tr, ti = c * or_ + s * oi, c * oi - s * or_

        def plus(a, b):
            return b if a is None else a if b is None else a + b

        def minus(a, b):
            if b is None:
                return a
            return -b if a is None else a - b

        out[k] = (plus(er, tr), plus(ei, ti))
        if 4 * k == size:
            continue
        low = minus(ei, ti)
        out[size // 2 - k] = (minus(er, tr), None if low is None else -low)
    return out


def short_dfts(n, k, incoming, mean_ref, taper_ref, wide, lhs):
    for c in range(4):
        wide[k * 4 + c] = incoming[k, :, :, c * 128 : (c + 1) * 128].astype(jnp.float32).reshape(n * RAD, 128)
    for c in range(4):
        w, half = c // 2, c % 2
        cols = slice(half * 128, (half + 1) * 128)
        xs = []
        for j in range(RAD):
            mean = mean_ref[j, :, c * 128 : (c + 1) * 128]
            xs.append((wide[k * 4 + c, pl.ds(j, n, stride=RAD), :] - mean) * taper_ref[j : j + 1, cols])
        bins = real_dft(xs)
        rows = slice((k * 2 + w) * n, (k * 2 + w + 1) * n)
        right = slice(T2 + half * 128, T2 + (half + 1) * 128)
        lhs[0, rows, cols] = bins[0][0].astype(jnp.bfloat16)
        lhs[0, rows, right] = bins[RAD // 2][0].astype(jnp.bfloat16)
        for g in range(1, RAD // 2):
            lhs[g, rows, cols] = bins[g][0].astype(jnp.bfloat16)
            lhs[g, rows, right] = bins[g][1].astype(jnp.bfloat16)


def whiten(n, caps, lhs, dft_ref, spec, white):
    power = jnp.zeros((lhs.shape[1], F2), jnp.float32)
    for g in range(RAD // 2):
        block = jnp.dot(lhs[g], dft_ref[g], preferred_element_type=jnp.float32)
        spec[g] = block
        for q in range(4):
            piece = block[:, q * F2 : (q + 1) * F2]
            power = power + piece * piece
    lane = lax.broadcasted_iota(jnp.int32, power.shape, 1)
    for step in (1, 2):
        low = (lane // step) % 2 == 0
        power = power + jnp.where(low, pltpu.roll(power, F2 - step, 1), pltpu.roll(power, step, 1))
    scale = 1.0 / jnp.sqrt(power * (1.0 / (2 * BAND)) + 1e-06)
    for g in range(RAD // 2):
        for q in range(4):
            piece = (spec[g, :, q * F2 : (q + 1) * F2] * scale).astype(jnp.bfloat16)
            at = g * BLK + q * F2
            for kw in range(2 * caps):
                k, w = kw // 2, kw % 2
                white[w, k * n : (k + 1) * n, at : at + F2] = piece[kw * n : (kw + 1) * n]


def pairs_kernel(n, white, pairs_ref, live_ref, lag_hbm, out_ref, cross, lag, lag_sem):
    lag_copy = pltpu.make_async_copy(lag_hbm, lag, lag_sem)
    lag_copy.start()
    caps = white.shape[1] // n
    wide = max(128, caps * n)
    pair_cap = pairs_ref.shape[1]
    row = lax.broadcasted_iota(jnp.int32, (wide, pair_cap), 0)
    slot = jnp.where(row < caps * n, (row % n) * caps + row // n, caps * n)
    alive = lax.broadcasted_iota(jnp.int32, (1, pair_cap), 1) < live_ref[0]
    hots = []
    for member in range(2):
        index = jnp.where(alive, pairs_ref[member : member + 1, :], -1)
        hot = jnp.where(slot == index, 1.0, 0.0).T
        hots.append(hot[:, : caps * n].astype(jnp.bfloat16))
    chunk = pair_cap
    for lo in range(0, pair_cap, chunk):
        hot_a, hot_b = hots[0][lo : lo + chunk], hots[1][lo : lo + chunk]
        for block in range(RAD):
            cols = slice(block * T2, (block + 1) * T2)
            real = imag = 0.0
            for w in range(2):
                a = jnp.dot(hot_a, white[w, :, cols], preferred_element_type=jnp.float32)
                b = jnp.dot(hot_b, white[w, :, cols], preferred_element_type=jnp.float32)
                ra, ia, rb, ib = a[:, :F2], a[:, F2:], b[:, :F2], b[:, F2:]
                real = real + (ra * rb + ia * ib)
                imag = imag + (ia * rb - ra * ib)
            cross[lo // chunk, :, block * T2 : block * T2 + F2] = (real * 0.5).astype(jnp.bfloat16)
            cross[lo // chunk, :, block * T2 + F2 : (block + 1) * T2] = (imag * 0.5).astype(jnp.bfloat16)
        if lo == 0:
            lag_copy.wait()
        out_ref[lo : lo + chunk, :] = jnp.dot(cross[lo // chunk], lag[...], preferred_element_type=jnp.float32)


def body(record, starts, send_rows, send_count, pair_slots, pair_count):
    local, windows = record.shape[0], starts.shape[0]
    n, caps = send_rows.shape[1], send_rows.shape[2]
    lanes = caps * windows * T2
    split = n // RAD
    width = windows * WLEN // n
    pair_cap = pair_slots.shape[1]
    f32, bf16 = jnp.float32, jnp.bfloat16
    vmem, smem = pl.BlockSpec(memory_space=pltpu.VMEM), pl.BlockSpec(memory_space=pltpu.SMEM)
    dma = pltpu.SemaphoreType.DMA
    hbm = pl.BlockSpec(memory_space=pl.ANY)
    rows_shape = (caps, n, RAD, windows * T2)
    part_shape = (n, 1, width)
    slab_shape = (RAD, 1, windows * T2)
    outgoing, part = pl.pallas_call(
        functools.partial(cut_kernel, n, split),
        out_shape=(jax.ShapeDtypeStruct(rows_shape, bf16), jax.ShapeDtypeStruct(part_shape, f32)),
        in_specs=[vmem, smem, vmem, vmem],
        out_specs=(vmem, vmem),
        scratch_shapes=[
            pltpu.VMEM((windows, local, WLEN), f32),
            pltpu.VMEM((lanes // 128, n * RAD, 128), f32),
            pltpu.VMEM(slab_shape, f32),
        ],
        compiler_params=pltpu.CompilerParams(vmem_limit_bytes=VMEM_LIMIT),
        name="cut",
    )(record, starts, send_rows[0].T, send_count)
    dft, lag, taper = tables()
    rows = caps * windows * n
    white = pl.pallas_call(
        functools.partial(exchange_kernel, n, split, local * n),
        out_shape=jax.ShapeDtypeStruct((windows, caps * n, 2 * F), bf16),
        in_specs=[vmem, vmem, vmem, hbm],
        out_specs=vmem,
        scratch_shapes=[
            pltpu.VMEM(rows_shape, bf16),
            pltpu.VMEM(part_shape, f32),
            pltpu.VMEM(part_shape, f32),
            pltpu.VMEM(slab_shape, f32),
            pltpu.VMEM((lanes // 128, n * RAD, 128), f32),
            pltpu.VMEM((RAD // 2, rows, BLK), bf16),
            pltpu.VMEM((RAD // 2, rows, BLK), f32),
            pltpu.VMEM(dft.shape, bf16),
            dma((caps * n,)), dma((caps * n,)), dma((n,)), dma((n,)), dma((n,)), dma((n,)), dma((caps,)), dma,
        ],
        compiler_params=pltpu.CompilerParams(
            collective_id=0, has_side_effects=True, vmem_limit_bytes=VMEM_LIMIT
        ),
        name="exchange",
    )(outgoing, part, jnp.asarray(taper), jnp.asarray(dft))
    return pl.pallas_call(
        functools.partial(pairs_kernel, n),
        out_shape=jax.ShapeDtypeStruct((pair_cap, LAGS), f32),
        in_specs=[vmem, vmem, smem, hbm],
        out_specs=vmem,
        scratch_shapes=[
            pltpu.VMEM((1, pair_cap, 2 * F), bf16),
            pltpu.VMEM(lag.shape, bf16),
            dma,
        ],
        compiler_params=pltpu.CompilerParams(vmem_limit_bytes=VMEM_LIMIT),
        name="pairs",
    )(white, pair_slots, pair_count, jnp.asarray(lag))


def solution(mesh):
    in_specs = (
        P(("groups", "chan"), None),
        P("groups"),
        P(("groups", "chan"), None, None),
        P(("groups", "chan"), None),
        P(None, ("groups", "chan")),
        P(("groups", "chan")),
    )
    out_specs = P(("groups", "chan"), None)
    return jax.shard_map(body, mesh=mesh, in_specs=in_specs, out_specs=out_specs, check_vma=False)
```
